256 devices in a mesh: cells: 64 (over y, z, core), rep: 4 (over x).
Axes of the slice: x: 4, y: 4, z: 8, core: 2. Of those that a mesh axis runs over, the one named last changes fastest.
Arguments:
- source: bfloat16 [98304, 256], P('cells'), may hold values from -24 to 24, as said below
- target: bfloat16 [524288, 256], P('cells'), may hold values from -24 to 24, as said below
- pairs: int32 [192, 32], P('cells', 'rep'), may hold values from 0 to 1023, as said below
- live: int32 [192], P('cells'), may hold values from 1 to 32, 3072 in all
Outputs:
- source_potential: float32 [98304], P('cells')
- target_potential: float32 [524288], P('cells')
The draws below stay inside these ranges and needn't reach their ends.
Inputs may be any that keep to these rules, and one draw needn't show every extreme that they name: `source`: rows are cell embeddings. `target`: rows are cell embeddings. `pairs`: block t is owned by cells index t // 16. The slots held by one device (the rows of one cells index and the 8 columns of one rep index) name distinct target blocks, at most 1 of them owned by any one cells index, and exactly 1 for some owner.
All inputs are finite; a program needn't handle non-finite values. No bound on the sum of `live` on one device may be relied on, other than what follows from the above.
Results may differ from the reference program's by a relative error of at most 0.0004.
Values may be sent and summed in bfloat16 or wider, within the bound.
No kernel may reach another device: no remote copies, remote signals or barrier semaphores. Data moves between devices by JAX's collectives and lax.ppermute only.
A program may use at most 128 MiB of HBM per device.

```python
import math
import jax
import jax.numpy as jnp
import numpy as np
from jax import lax

E = 256
BLK = 512
KC = 32
ITERS = 2
SB_DEV = 3
TB_DEV = 16
KR = 8
CAP = 1
NSB = 192
NTB = 1024
NS = 98304
NT = 524288
N_CELLS = 64
N_REP = 4


def embedding(key, count_rows):
    key_vals = jax.random.fold_in(key, 0)
    values = jnp.clip(jax.random.normal(key_vals, (count_rows, E), jnp.float32), -6.0, 6.0)
    return values


def draw_source(key, part):
    key = jax.random.fold_in(key, 11)
    return embedding(key, NS).astype(jnp.bfloat16)


def draw_target(key, part):
    key = jax.random.fold_in(key, 23)
    return embedding(key, NT).astype(jnp.bfloat16)


def device_slots(key):
    key_one, key_two, key_three, key_four = jax.random.split(key, 4)
    tickets_all = N_CELLS * CAP
    tickets = jnp.arange(tickets_all, dtype=jnp.int32)
    shuffled = jax.random.permutation(key_one, tickets_all)
    position = jnp.argsort(shuffled).astype(jnp.int32)
    forced = jax.random.randint(key_two, (), 0, N_CELLS)
    ordering = position + jnp.where(tickets // CAP == forced, 0, tickets_all)
    chosen = jnp.argsort(ordering)[:SB_DEV * KR].astype(jnp.int32)
    chosen = chosen[jax.random.permutation(key_three, SB_DEV * KR)]
    owner_of = chosen // CAP
    rank_of = chosen % CAP
    block_perm = jax.vmap(lambda owner_at: jax.random.permutation(jax.random.fold_in(key_four, owner_at), TB_DEV))(jnp.arange(N_CELLS))
    picked = block_perm[owner_of, rank_of].astype(jnp.int32)
    return (owner_of * TB_DEV + picked).reshape(SB_DEV, KR)


def draw_pairs(key, part):
    key = jax.random.fold_in(key, 5)
    device_keys = jax.vmap(lambda number: jax.random.fold_in(key, number))(jnp.arange(N_CELLS * N_REP))
    slots_all = jax.vmap(device_slots)(device_keys)
    slots_all = slots_all.reshape(N_CELLS, N_REP, SB_DEV, KR).transpose(0, 2, 1, 3)
    return slots_all.reshape(NSB, KC).astype(jnp.int32)


def split_up(amount, total, reach, lean):
    weights = [(1 << 20) // math.isqrt(grade ** lean) + 1 for grade in range(2, amount + 1)]
    surplus, holding = total - reach - (amount - 1), [1] * (amount - 1)
    while surplus > 0:
        free = [i for i in range(amount - 1) if holding[i] < reach]
        pool, left = sum([weights[i] for i in free]), surplus
        for i in free:
            addition = min(reach - holding[i], max(1, left * weights[i] // pool), surplus)
            holding[i] = holding[i] + addition
            surplus = surplus - addition
    return np.array([reach] + holding)


def uneven_parts(own_key, amount, total, limit, slope):
    if amount == 2:
        one = jax.random.randint(own_key, (), max(1, total - limit), min(limit, total - 1) + 1)
        return jnp.stack([one, total - one])
    sizes = jnp.asarray(split_up(amount, total, limit, slope), jnp.int32)
    pairs = (amount - 1) // 2
    giver, sink = sizes[1:1 + 2 * pairs:2], sizes[2:2 + 2 * pairs:2]
    slack = jnp.minimum(giver - 1, limit - sink)
    passed = jax.random.randint(jax.random.fold_in(own_key, 1), (pairs,), 0, 1 << 20) % (slack + 1)
    sizes = sizes.at[1:1 + 2 * pairs:2].set(giver - passed).at[2:2 + 2 * pairs:2].set(sink + passed)
    return sizes[jax.random.permutation(jax.random.fold_in(own_key, 2), amount)]


def setup_inputs(seed: int = 0) -> dict:
    splits = jax.random.split(jax.random.key(seed), 5)
    source = draw_source(jax.random.fold_in(splits[4], 71), 0)
    target = draw_target(jax.random.fold_in(splits[4], 71), 0)
    pairs = draw_pairs(jax.random.fold_in(splits[4], 71), 0)
    live = uneven_parts(splits[3], NSB, NSB * KC // 2, KC, 1).astype(jnp.int32)
    return dict(source=source, target=target, pairs=pairs, live=live)


LOWEST = -1e+30
DUSTBIN = -1.0

def reference(source, target, pairs, live):
    epsilon = math.sqrt(2.0 * E)
    src_blocks = source.reshape(NSB, BLK, E)
    tgt_blocks = target.reshape(NTB, BLK, E)
    live_slot = jnp.arange(KC, dtype=jnp.int32)[None, :] < live[:, None]

    def tiles(args):
        rows_x, block_ids = args
        partner = tgt_blocks[block_ids].astype(jnp.float32)
        own = rows_x.astype(jnp.float32)
        inner = jnp.einsum('ie,kje->kij', own, partner, precision=lax.Precision.HIGHEST)
        sq_own = lax.optimization_barrier(jnp.sum(own * own, axis=1))
        sq_partner = lax.optimization_barrier(jnp.sum(partner * partner, axis=2))
        return sq_own[None, :, None] + sq_partner[:, None, :] - 2.0 * inner
    cost = lax.map(tiles, (src_blocks, pairs))
    flat_ids = pairs.reshape(NSB * KC)
    potential_g = jnp.zeros((NTB, BLK), jnp.float32)
    potential_f = jnp.zeros((NSB, BLK), jnp.float32)

    def row(args):
        tile, g_part, keep = args
        score = jnp.where(keep[:, None, None], (g_part[:, None, :] - tile) / epsilon, LOWEST)
        largest = lax.optimization_barrier(jnp.max(score, axis=(0, 2)))
        summed = lax.optimization_barrier(jnp.sum(jnp.where(keep[:, None, None], jnp.exp(score - largest[None, :, None]), 0.0), axis=(0, 2)))
        return -epsilon * (largest + jnp.log(summed))

    def column(args):
        tile, f_row, keep = args
        score = jnp.where(keep[:, None, None], (f_row[None, :, None] - tile) / epsilon, LOWEST)
        largest = lax.optimization_barrier(jnp.max(score, axis=1))
        summed = lax.optimization_barrier(jnp.sum(jnp.where(keep[:, None, None], jnp.exp(score - largest[:, None, :]), 0.0), axis=1))
        return (largest, summed)
    for iteration in range(ITERS):
        potential_f = lax.map(row, (cost, potential_g[pairs], live_slot))
        col_max, col_sum = lax.map(column, (cost, potential_f, live_slot))
        col_max = col_max.reshape(NSB * KC, BLK)
        col_sum = col_sum.reshape(NSB * KC, BLK)
        block_max = jnp.full((NTB, BLK), LOWEST, jnp.float32).at[flat_ids].max(col_max)
        block_sum = jnp.zeros((NTB, BLK), jnp.float32).at[flat_ids].add(col_sum * jnp.exp(col_max - block_max[flat_ids]))
        merged_max = jnp.maximum(block_max, DUSTBIN)
        merged_sum = block_sum * jnp.exp(block_max - merged_max) + jnp.exp(DUSTBIN - merged_max)
        potential_g = -epsilon * (merged_max + jnp.log(merged_sum))
    return (potential_f.reshape(NS), potential_g.reshape(NT))
```

```python
import functools
import math

import jax
import jax.numpy as jnp
from jax import lax
from jax.experimental import pallas as pl
from jax.experimental.pallas import tpu as pltpu
from jax.sharding import PartitionSpec as P

DUSTBIN = -1.0
LOWEST = -1e30

NY, NZ, NCORE, NREP = 4, 8, 2, 4
SB, TB, KR, BLK, E = 3, 16, 8, 512, 256
ROWS = BLK // NREP
HALF = ROWS // 2
NSRC = NY * NZ * SB
NTGT = NCORE * TB
NSLOT = NY * NZ * NREP * NCORE
AT_COUNT, AT_CORE, LIST = NSLOT, NSLOT + 1, NSLOT + 128
OUT_BUFS, IN_BUFS = 8, 32
MIB = 1 << 20


def cell(y, z, core):
    return ((y % NY) * NZ + z % NZ) * NCORE + core


def plane_shift(a, dy, dz):
    perm = [
        (cell(y, z, c), cell(y + dy, z + dz, c))
        for y in range(NY) for z in range(NZ) for c in range(NCORE)
    ]
    return lax.ppermute(a, "cells", perm)


def other_core(a):
    return lax.ppermute(a, "cells", [(i, i ^ 1) for i in range(NY * NZ * NCORE)])


def rep_shift(a, k):
    return lax.ppermute(a, "rep", [(i, (i + k) % NREP) for i in range(NREP)])


def from_reps(a):
    return [a] + [rep_shift(a, k) for k in range(1, NREP)]


def sum_reps(a):
    p = from_reps(a)
    return (p[0] + p[2]) + (p[1] + p[3])


def join_plane(a, join):
    a = join([a] + [plane_shift(a, k, 0) for k in range(1, NY)])
    return join([a] + [plane_shift(a, 0, k) for k in range(1, NZ)])


def join_lse(parts):
    top = functools.reduce(jnp.maximum, parts)
    return top + jnp.log(sum(jnp.exp(p - top) for p in parts))


def gather_rows(xs):
    a, b = xs[:, :HALF], xs[:, HALF:]
    up, down = [a], [a]
    ycat = jnp.stack([b, plane_shift(b, 1, 0), plane_shift(b, 2, 0), plane_shift(b, 3, 0)])
    for k in range(1, 5):
        up.append(plane_shift(up[-1], 0, 1))
        if k < 4:
            down.append(plane_shift(down[-1], 0, -1))
    zcat = jnp.stack(up + [down[3], down[2], down[1]])
    y1, y3 = plane_shift(zcat, 1, 0), plane_shift(zcat, -1, 0)
    y2a, y2b = plane_shift(y1[:4], 1, 0), plane_shift(y3[4:], -1, 0)
    z1, z7 = plane_shift(ycat, 0, 1), plane_shift(ycat, 0, -1)
    z2, z6 = plane_shift(z1, 0, 1), plane_shift(z7, 0, -1)
    z3, z5 = plane_shift(z2, 0, 1), plane_shift(z6, 0, -1)
    z4a, z4b = plane_shift(z3[:2], 0, 1), plane_shift(z5[2:], 0, -1)
    return [zcat, y1, y3, y2a, y2b, ycat, z1, z2, z3, z5, z6, z7, z4a, z4b]


def places(buf):
    lo, hi = pl.ds(0, HALF), pl.ds(HALF, HALF)
    out = [buf.at[dy, :, :, lo] for dy in (0, 1, 3)]
    out += [buf.at[2, pl.ds(0, 4), :, lo], buf.at[2, pl.ds(4, 4), :, lo]]
    out += [buf.at[:, dz, :, hi] for dz in (0, 1, 2, 3, 5, 6, 7)]
    out += [buf.at[pl.ds(0, 2), 4, :, hi], buf.at[pl.ds(2, 2), 4, :, hi]]
    return out


def slot_list(masked, at_y, at_z, chip, core):
    local = masked - chip * NTGT
    block = lax.broadcasted_iota(jnp.int32, masked.shape, 3)
    dz = lax.broadcasted_iota(jnp.int32, masked.shape, 0)
    dy = lax.broadcasted_iota(jnp.int32, masked.shape, 1)
    own = (((at_y - dy) % NY) * NZ + (at_z - dz) % NZ) * SB + block
    code = ((((dy * NZ + dz) * 4 + block) * NTGT + local) * 128) + own + 1
    found = []
    for owner in range(NCORE):
        hit = (local >= owner * TB) & (local < (owner + 1) * TB)
        found.append(jnp.sum(jnp.where(hit, code, 0), axis=(3, 4)))
    found = jnp.stack(found, axis=-1).reshape(NSLOT)
    valid = found > 0
    counter = jnp.arange(NSLOT, dtype=jnp.int32)
    place = jnp.sum((valid[None, :] & (counter[None, :] < counter[:, None])).astype(jnp.int32), axis=1)
    chosen = valid[None, :] & (place[None, :] == counter[:, None])
    codes = jnp.sum(jnp.where(chosen, found[None, :] - 1, 0), axis=1)
    count = jnp.sum(valid.astype(jnp.int32))
    tail = jnp.zeros((LIST - NSLOT,), jnp.int32).at[0].set(count).at[1].set(core)
    return jnp.concatenate([codes, tail]), (codes & 127).reshape(2, 128)


def lanes():
    return lax.broadcasted_iota(jnp.int32, (ROWS, 128), 1)


def column(a, at):
    return jnp.sum(jnp.where(lanes() == at, a, 0.0), axis=1, keepdims=True)


def tiles_kernel(scale, slots, y_own, y_other, sq, *refs):
    xs, (p_out, m_out, lse_out, xbuf, ybuf, pbuf, top, total, sem, p_sem) = refs[:14], refs[14:]
    core = slots[AT_CORE]
    count = slots[AT_COUNT]
    copies = [
        pltpu.make_async_copy(y_own, ybuf.at[pl.ds(core * TB, TB)], sem.at[0]),
        pltpu.make_async_copy(y_other, ybuf.at[pl.ds((1 - core) * TB, TB)], sem.at[1]),
    ]
    for i, (x, place) in enumerate(zip(xs, places(xbuf))):
        copies.append(pltpu.make_async_copy(x, place, sem.at[2 + i]))
    for copy in copies:
        copy.start()
    top[...] = jnp.full_like(top, LOWEST)
    total[...] = jnp.zeros_like(total)
    m_out[...] = jnp.zeros_like(m_out)
    for copy in copies:
        copy.wait()

    def out_copy(n):
        at = lax.rem(n, OUT_BUFS)
        return pltpu.make_async_copy(pbuf.at[at], p_out.at[n], p_sem.at[at])

    def step(n, carry):
        code = slots[n]
        own, t, block = code & 127, (code >> 7) & 31, (code >> 12) & 3
        dz, dy = (code >> 14) & 7, code >> 17
        inner = lax.dot_general(
            xbuf[dy, dz, block], ybuf[t], (((1,), (1,)), ((), ())),
            preferred_element_type=jnp.float32,
        )
        score = inner * scale - sq[pl.ds(t, 1), :]
        high = jnp.max(score, axis=1, keepdims=True)
        weight = jnp.exp(score - high)
        part = jnp.sum(weight, axis=1, keepdims=True)

        @pl.when(n >= OUT_BUFS)
        def _():
            out_copy(n - OUT_BUFS).wait()

        pbuf[lax.rem(n, OUT_BUFS)] = weight
        out_copy(n).start()
        at = n // 128
        m_out[at] = jnp.where(lanes() == n % 128, high, m_out[at])
        before = top[...]
        after = jnp.maximum(before, high)
        mine = lanes() == own
        total[...] = jnp.where(
            mine, total[...] * jnp.exp(before - after) + part * jnp.exp(high - after), total[...]
        )
        top[...] = jnp.where(mine, after, before)
        return carry

    lax.fori_loop(0, count, step, 0)

    def drain(n, carry):
        out_copy(n).wait()
        return carry

    lax.fori_loop(jnp.maximum(count - OUT_BUFS, 0), count, drain, 0)
    some = total[...] > 0.0
    lse = jnp.where(some, top[...] + jnp.log(jnp.where(some, total[...], 1.0)), LOWEST)
    lse_out[...] = lse.T


def stream(slots, p_ref, buf, sem, use):
    count = slots[AT_COUNT]

    def copy(n):
        at = lax.rem(n, IN_BUFS)
        return pltpu.make_async_copy(p_ref.at[n], buf.at[at], sem.at[at])

    def start(n, carry):
        copy(n).start()
        return carry

    lax.fori_loop(0, jnp.minimum(count, IN_BUFS), start, 0)

    def step(n, carry):
        code = slots[n]
        copy(n).wait()
        use(n, buf[lax.rem(n, IN_BUFS)], code & 127, (code >> 7) & 31)

        @pl.when(n + IN_BUFS < count)
        def _():
            copy(n + IN_BUFS).start()

        return carry

    lax.fori_loop(0, count, step, 0)


def add_column(col, alpha):
    def use(n, tile, own, t):
        weight = column(alpha[n // 128], n % 128)
        col[pl.ds(t, 1), :] += jnp.sum(tile * weight, axis=0, keepdims=True)

    return use


def by_slot(table, owns, at):
    return jnp.take_along_axis(table, jnp.broadcast_to(owns[pl.ds(at, 1), :], (ROWS, 128)), axis=1)


def first_columns_kernel(slots, owns, potential, m_in, p_ref, col, alpha, buf, sem):
    table = potential[...].T
    for at in range(2):
        alpha[at] = jnp.exp(m_in[at] + by_slot(table, owns, at))
    col[...] = jnp.zeros_like(col)
    stream(slots, p_ref, buf, sem, add_column(col, alpha))


def rows_kernel(slots, weights, alpha, p_ref, row_out, acc, buf, sem):
    acc[...] = jnp.zeros_like(acc)

    def use(n, tile, own, t):
        weight = column(alpha[n // 128], n % 128)
        part = jnp.sum(tile * weights[pl.ds(t, 1), :], axis=1, keepdims=True) * weight
        acc[...] += jnp.where(lanes() == own, part, 0.0)

    stream(slots, p_ref, buf, sem, use)
    row_out[...] = acc[...].T


def last_columns_kernel(slots, owns, row_sum, alpha, p_ref, col, beta, buf, sem):
    table = row_sum[...].T
    for at in range(2):
        beta[at] = alpha[at] / by_slot(table, owns, at)
    col[...] = jnp.zeros_like(col)
    stream(slots, p_ref, buf, sem, add_column(col, beta))


SMEM = pl.BlockSpec(memory_space=pltpu.SMEM)
VMEM = pl.BlockSpec(memory_space=pltpu.VMEM)
ANY = pl.BlockSpec(memory_space=pl.ANY)


def f32(*shape):
    return jax.ShapeDtypeStruct(shape, jnp.float32)


def call(kernel, ins, outs, out_specs, scratch, limit):
    return pl.pallas_call(
        kernel,
        in_specs=ins,
        out_specs=out_specs,
        out_shape=outs,
        scratch_shapes=scratch,
        compiler_params=pltpu.CompilerParams(vmem_limit_bytes=limit * MIB),
    )


def stream_scratch():
    return [pltpu.VMEM((IN_BUFS, ROWS, BLK), jnp.float32), pltpu.SemaphoreType.DMA((IN_BUFS,))]


def padded(rows):
    return jnp.concatenate([rows, jnp.ones((128 - NSRC, ROWS), jnp.float32)], axis=0)


def body(source, target, pairs, live):
    cells, rep = lax.axis_index("cells"), lax.axis_index("rep")
    core, chip = cells % NCORE, cells // NCORE
    at_y, at_z = chip // NZ, chip % NZ
    epsilon = math.sqrt(2.0 * E)

    own_rows = lax.dynamic_index_in_dim(source.reshape(SB, NREP, ROWS, E), rep, 1, False)
    gathered = gather_rows(own_rows)

    own_targets = target.reshape(TB, BLK, E)
    other_targets = other_core(own_targets)
    wide = own_targets.astype(jnp.float32)
    sq_own = jnp.sum(wide * wide, axis=2) / epsilon
    sq_other = other_core(sq_own)
    sq = jnp.where(
        core == 0, jnp.concatenate([sq_own, sq_other]), jnp.concatenate([sq_other, sq_own])
    )
    wide = own_rows.astype(jnp.float32)
    sq_rows = jnp.sum(wide * wide, axis=2)

    slot = rep * KR + jnp.arange(KR, dtype=jnp.int32)
    masked = jnp.where(slot[None, :] < live[:, None], pairs, -1).reshape(1, SB * KR)
    masked = jnp.concatenate(from_reps(masked), axis=1)
    masked = jnp.concatenate([masked] + [plane_shift(masked, k, 0) for k in range(1, NY)], axis=0)
    masked = jnp.stack([masked] + [plane_shift(masked, 0, k) for k in range(1, NZ)])
    slots, owns = slot_list(masked.reshape(NZ, NY, NREP, SB, KR), at_y, at_z, chip, core)

    tiles, tops, lse = call(
        functools.partial(tiles_kernel, 2.0 / epsilon),
        [SMEM, ANY, ANY, VMEM] + [ANY] * 14,
        [f32(NSLOT, ROWS, BLK), f32(2, ROWS, 128), f32(128, ROWS)],
        [ANY, VMEM, VMEM],
        [
            pltpu.VMEM((NY, NZ, SB, ROWS, E), jnp.bfloat16),
            pltpu.VMEM((NTGT, BLK, E), jnp.bfloat16),
            pltpu.VMEM((OUT_BUFS, ROWS, BLK), jnp.float32),
            pltpu.VMEM((ROWS, 128), jnp.float32),
            pltpu.VMEM((ROWS, 128), jnp.float32),
            pltpu.SemaphoreType.DMA((16,)),
            pltpu.SemaphoreType.DMA((OUT_BUFS,)),
        ],
        40,
    )(slots, own_targets, other_targets, sq, *gathered)

    potential = -join_plane(lse[:NSRC], join_lse)

    col, alpha = call(
        first_columns_kernel,
        [SMEM, VMEM, VMEM, VMEM, ANY],
        [f32(NTGT, BLK), f32(2, ROWS, 128)],
        [VMEM, VMEM],
        stream_scratch(),
        24,
    )(slots, owns, padded(potential), tops, tiles)
    col = sum_reps(col + other_core(col))
    weights = 1.0 / (col + math.exp(DUSTBIN))

    row_sum = call(
        rows_kernel,
        [SMEM, VMEM, VMEM, ANY],
        f32(128, ROWS),
        VMEM,
        [pltpu.VMEM((ROWS, 128), jnp.float32)] + stream_scratch(),
        24,
    )(slots, weights, alpha, tiles)
    row_sum = join_plane(row_sum[:NSRC], sum)

    col = call(
        last_columns_kernel,
        [SMEM, VMEM, VMEM, VMEM, ANY],
        f32(NTGT, BLK),
        VMEM,
        [pltpu.VMEM((2, ROWS, 128), jnp.float32)] + stream_scratch(),
        24,
    )(slots, owns, padded(row_sum), alpha, tiles)

    mine = lax.dynamic_slice_in_dim(potential, chip * SB, SB, 0)
    mine = mine - jnp.log(lax.dynamic_slice_in_dim(row_sum, chip * SB, SB, 0))
    f_part = epsilon * mine + sq_rows
    parts = jnp.stack(from_reps(f_part))
    f_out = jnp.stack(
        [lax.dynamic_index_in_dim(parts, (rep - j) % NREP, 0, False) for j in range(NREP)], axis=1
    )

    halves = col.reshape(NCORE, TB, BLK)
    keep = lax.dynamic_index_in_dim(halves, core, 0, False)
    give = lax.dynamic_index_in_dim(halves, 1 - core, 0, False)
    col = sum_reps(keep + other_core(give))
    g_out = -epsilon * jnp.log(col + math.exp(DUSTBIN))
    return f_out.reshape(-1), g_out.reshape(-1)


def solution(mesh):
    in_specs = (P("cells", None), P("cells", None), P("cells", "rep"), P("cells"))
    out_specs = (P("cells"), P("cells"))
    return jax.shard_map(body, mesh=mesh, in_specs=in_specs, out_specs=out_specs, check_vma=False)
```

```python
import functools
import math

import jax
import jax.numpy as jnp
from jax import lax
from jax.experimental import pallas as pl
from jax.experimental.pallas import tpu as pltpu
from jax.sharding import PartitionSpec as P

DUSTBIN = -1.0
LOWEST = -1e30

NY, NZ, NCORE, NREP = 4, 8, 2, 4
SB, TB, KR, BLK, E = 3, 16, 8, 512, 256
ROWS = BLK // NREP
HALF = ROWS // 2
NSRC = NY * NZ * SB
NTGT = NCORE * TB
NSLOT = NY * NZ * NREP * NCORE
AT_COUNT, LIST = NSLOT, NSLOT + 128
OUT_PAIRS, IN_BUFS, GROUP = 4, 32, 4
NOTE = 16
MIB = 1 << 20
EARLY_Y, EARLY_Z = (0, 1, 3), (0, 1, 2, 3, 5, 6, 7)


def cell(y, z, core):
    return ((y % NY) * NZ + z % NZ) * NCORE + core


def plane_shift(a, dy, dz):
    perm = [
        (cell(y, z, c), cell(y + dy, z + dz, c))
        for y in range(NY) for z in range(NZ) for c in range(NCORE)
    ]
    return lax.ppermute(a, "cells", perm)


def other_core(a):
    return lax.ppermute(a, "cells", [(i, i ^ 1) for i in range(NY * NZ * NCORE)])


def rep_shift(a, k):
    return lax.ppermute(a, "rep", [(i, (i + k) % NREP) for i in range(NREP)])


def from_reps(a):
    return [a] + [rep_shift(a, k) for k in range(1, NREP)]


def sum_reps(a):
    p = from_reps(a)
    return (p[0] + p[2]) + (p[1] + p[3])


def join_plane(a, join):
    a = join([a] + [plane_shift(a, k, 0) for k in range(1, NY)])
    a = join([a, plane_shift(a, 0, 1)])
    return join([a] + [plane_shift(a, 0, k) for k in range(2, NZ, 2)])


def join_lse(parts):
    top = functools.reduce(jnp.maximum, parts)
    return top + jnp.log(sum(jnp.exp(p - top) for p in parts))


def gather_rows(xs, note):
    a = xs[:, :HALF].reshape(SB * HALF, E)
    b = jnp.concatenate([xs[:, HALF:].reshape(SB * HALF, E), note])
    up, down = [a], [a]
    for k in range(1, 5):
        up.append(plane_shift(up[-1], 0, 1))
        if k < 4:
            down.append(plane_shift(down[-1], 0, -1))
    after = (up[4][0, 0] + down[3][0, 0]) * 0
    ycat = jnp.stack([b, plane_shift(b, 1, 0), plane_shift(b, 2, 0), plane_shift(b, 3, 0)]) + after
    zcat = jnp.stack(up + [down[3], down[2], down[1]])
    y1, y3 = plane_shift(zcat, 1, 0), plane_shift(zcat, -1, 0)
    z1, z7 = plane_shift(ycat, 0, 1), plane_shift(ycat, 0, -1)
    z2, z6 = plane_shift(z1, 0, 1), plane_shift(z7, 0, -1)
    z3, z5 = plane_shift(z2, 0, 1), plane_shift(z6, 0, -1)
    y2a, y2b = plane_shift(y1[:4], 1, 0), plane_shift(y3[4:], -1, 0)
    z4a, z4b = plane_shift(z3[:2], 0, 1), plane_shift(z5[2:], 0, -1)
    return [zcat, y1, y3, ycat, z1, z2, z3, z5, z6, z7], [y2a, y2b, z4a, z4b]


def pieces(early, late, first):
    a_rows, b_rows = dict(zip(EARLY_Y, early)), dict(zip(EARLY_Z, early[3:]))
    out = []
    if first:
        out += [(a_rows[dy], pl.ds(0, NY), dy, None, False) for dy in ()]
        for dy in EARLY_Y:
            out += [(a_rows[dy].at[pl.ds(0, 4)], dy, pl.ds(0, 4), False)]
            out += [(a_rows[dy].at[pl.ds(5, 3)], dy, pl.ds(5, 3), False)]
        for dz in EARLY_Z:
            out += [(b_rows[dz].at[pl.ds(0, 2)], pl.ds(0, 2), dz, True)]
            out += [(b_rows[dz].at[pl.ds(3, 1)], pl.ds(3, 1), dz, True)]
        return out
    out += [(late[0], 2, pl.ds(0, 4), False), (late[1], 2, pl.ds(4, 4), False)]
    out += [(a_rows[dy].at[pl.ds(4, 1)], dy, pl.ds(4, 1), False) for dy in EARLY_Y]
    out += [(b_rows[dz].at[pl.ds(2, 1)], pl.ds(2, 1), dz, True) for dz in EARLY_Z]
    out += [(late[2], pl.ds(0, 2), 4, True), (late[3], pl.ds(2, 2), 4, True)]
    return out


def note_row(masked):
    named = masked.reshape(SB * KR, 1)
    block = (jnp.arange(SB * KR, dtype=jnp.int32) // KR)[:, None]
    owner = jnp.arange(NY * NZ * NCORE, dtype=jnp.int32)[None, :]
    hit = (named >= owner * TB) & (named < (owner + 1) * TB)
    return jnp.sum(jnp.where(hit, 1 + TB * block + named - owner * TB, 0), axis=0, keepdims=True)


def lanes():
    return lax.broadcasted_iota(jnp.int32, (ROWS, 128), 1)


def lane_of(a, at):
    return jnp.take_along_axis(a, jnp.full((ROWS, 128), at, jnp.int32), axis=1)


def tiles_kernel(scale, first, here, sq, y_own, y_other, *refs):
    if first:
        early, late, before = refs[:10], [], None
        refs = refs[10:]
    else:
        early, late, before = refs[:10], refs[10:14], refs[14:20]
        refs = refs[20:]
    slots, owns, p_out, m_out, l_out, top = refs[:6]
    refs = refs[6:]
    if not first:
        lse_out, refs = refs[0], refs[1:]
    xbuf, ybuf, even, odd, pbuf, mbuf, found, found_s, sem, p_sem = refs
    chip, core, at_y, at_z = here[0], here[1], here[2], here[3]

    note_copies = []
    if first:
        for i, dz in enumerate(EARLY_Z):
            note_copies.append((early[3 + i].at[:, pl.ds(SB * HALF, NOTE)], mbuf.at[dz]))
    else:
        for i, dz in enumerate(EARLY_Z):
            note_copies.append((early[3 + i].at[pl.ds(2, 1), pl.ds(SB * HALF, NOTE)], mbuf.at[dz, pl.ds(2, 1)]))
        note_copies.append((late[2].at[:, pl.ds(SB * HALF, NOTE)], mbuf.at[4, pl.ds(0, 2)]))
        note_copies.append((late[3].at[:, pl.ds(SB * HALF, NOTE)], mbuf.at[4, pl.ds(2, 2)]))
    note_copies = [
        pltpu.make_async_copy(src, dst, sem.at[i]) for i, (src, dst) in enumerate(note_copies)
    ]
    copies = [
        pltpu.make_async_copy(y_own, ybuf.at[pl.ds(core * TB, TB)], sem.at[10]),
        pltpu.make_async_copy(y_other, ybuf.at[pl.ds((1 - core) * TB, TB)], sem.at[11]),
    ]
    at = 12
    for src, dy, dz, second in pieces(early, late, first):
        for block in range(SB):
            rows = pl.ds(HALF if second else 0, HALF)
            part = src.at[:, pl.ds(block * HALF, HALF)]
            copies.append(pltpu.make_async_copy(part, xbuf.at[dy, dz, block, rows], sem.at[at]))
            at += 1
    for copy in note_copies + copies:
        copy.start()
    if first:
        top[...] = jnp.full_like(top, LOWEST)
        m_out[...] = jnp.zeros_like(m_out)
        l_out[...] = jnp.zeros_like(l_out)
        owns[...] = jnp.zeros_like(owns)
        begin = jnp.int32(0)
    else:
        slots_in, owns_in, _, m_in, l_in, top_in = before
        top[...], m_out[...], l_out[...], owns[...] = top_in[...], m_in[...], l_in[...], owns_in[...]
        begin = slots_in[AT_COUNT]

        def keep(n, carry):
            slots[n] = slots_in[n]
            return carry

        lax.fori_loop(0, begin, keep, 0)
    for copy in note_copies:
        copy.wait()

    source_lane = lax.broadcasted_iota(jnp.int32, (E, 128), 0)
    lane = lax.broadcasted_iota(jnp.int32, (E, 128), 1)
    wanted = (lane < NREP * NCORE) & (
        source_lane == (lane >> 1) * (NY * NZ * NCORE) + chip * NCORE + (lane & 1)
    )
    picked = lax.dot_general(
        mbuf[...].reshape(NY * NZ * NOTE, E), wanted.astype(jnp.bfloat16), (((1,), (0,)), ((), ())),
        preferred_element_type=jnp.float32,
    )
    found[...] = picked.reshape(NY * NZ, NOTE, 128)[:, 0].astype(jnp.int32)
    move = pltpu.make_async_copy(found, found_s, sem.at[at])
    move.start()
    move.wait()

    def of_chip(dz, dy, n):
        base = (((at_y - dy) & (NY - 1)) * NZ + ((at_z - dz) & (NZ - 1))) * SB
        where = (dy << 5) | (dz << 2)
        for j in range(NREP * NCORE):
            value = found_s[dz * NY + dy, j] - 1
            block = value >> 4
            t = (value & (TB - 1)) + (j & 1) * TB
            slots[n] = ((where | block) << 12) | (t << 7) | (base + block)
            n = n + (value >= 0).astype(jnp.int32)
        return n

    count = begin
    if first:
        for dz in EARLY_Z:
            for dy in EARLY_Y:
                count = of_chip(dz, dy, count)
    else:
        for dz in range(NZ):
            count = of_chip(dz, 2, count)
        for dy in EARLY_Y:
            count = of_chip(4, dy, count)
    slots[AT_COUNT] = count
    for copy in copies:
        copy.wait()

    def score(n, into):
        code = slots[jnp.minimum(n, count - 1)]
        t, block, dz, dy = (code >> 7) & 31, (code >> 12) & 3, (code >> 14) & 7, (code >> 17) & 3
        inner = lax.dot_general(
            xbuf[dy, dz, block], ybuf[t], (((1,), (1,)), ((), ())),
            preferred_element_type=jnp.float32,
        )
        into[...] = inner * scale - sq[pl.ds(t, 1), :]

    def weigh(n, source, into):
        own = slots[jnp.minimum(n, count - 1)] & 127
        values = source[...]
        high = jnp.max(values, axis=1, keepdims=True)
        weight = jnp.exp(values - high)
        into[...] = weight
        part = jnp.sum(weight, axis=1, keepdims=True)
        half, mine = n // 128, lanes() == n % 128
        m_out[half] = jnp.where(mine, high, m_out[half])
        l_out[half] = jnp.where(mine, part, l_out[half])
        owns[half] = jnp.where(mine[:8], own, owns[half])
        top[...] = jnp.where(lanes() == own, jnp.maximum(top[...], high), top[...])

    def out_copy(n, k, ring):
        return pltpu.make_async_copy(pbuf.at[ring, k], p_out.at[n], p_sem.at[ring, k])

    @pl.when(count > begin)
    def _():
        score(begin, even)

    def step(i, carry):
        n, ring = begin + 2 * i, lax.rem(i, OUT_PAIRS)

        @pl.when(i >= OUT_PAIRS)
        def _():
            for k in range(2):
                out_copy(n - 2 * OUT_PAIRS + k, k, ring).wait()

        score(n + 1, odd)
        weigh(n, even, pbuf.at[ring, 0])
        score(n + 2, even)

        @pl.when(n + 1 < count)
        def _():
            weigh(n + 1, odd, pbuf.at[ring, 1])

        for k in range(2):

            @pl.when(n + k < count)
            def _():
                out_copy(n + k, k, ring).start()

        return carry

    pairs = (count - begin + 1) // 2
    lax.fori_loop(0, pairs, step, 0)

    def drain(i, carry):
        n = begin + 2 * i
        for k in range(2):

            @pl.when(n + k < count)
            def _():
                out_copy(n + k, k, lax.rem(i, OUT_PAIRS)).wait()

        return carry

    lax.fori_loop(jnp.maximum(pairs - OUT_PAIRS, 0), pairs, drain, 0)
    if first:
        return
    total = jnp.zeros((ROWS, 128), jnp.float32)
    for half in range(2):
        live = lanes() + half * 128 < count
        scaled = l_out[half] * jnp.exp(m_out[half] - by_slot(top[...], owns, half))
        own_rows = lax.broadcasted_iota(jnp.int32, (128, 128), 0)
        one_hot = (own_rows == owns[half, pl.ds(0, 1), :]).astype(jnp.float32)
        total = total + lax.dot_general(
            jnp.where(live, scaled, 0.0), one_hot, (((1,), (1,)), ((), ())),
            precision=lax.Precision.HIGHEST, preferred_element_type=jnp.float32,
        )
    some = total > 0.0
    lse = jnp.where(some, top[...] + jnp.log(jnp.where(some, total, 1.0)), LOWEST)
    lse_out[...] = lse.T


def stream(slots, p_ref, buf, sem, use):
    count = slots[AT_COUNT]

    def copy(n):
        at = lax.rem(n, IN_BUFS)
        return pltpu.make_async_copy(p_ref.at[n], buf.at[at], sem.at[at])

    def start(n, carry):
        copy(n).start()
        return carry

    lax.fori_loop(0, jnp.minimum(count, IN_BUFS), start, 0)

    def step(i, carry):
        n = i * GROUP
        for k in range(GROUP):

            @pl.when(n + k < count)
            def _():
                copy(n + k).wait()

        group = []
        for k in range(GROUP):
            at = jnp.minimum(n + k, count - 1)
            on = jnp.where(n + k < count, 1.0, 0.0)
            code = slots[at]
            group.append((at, on, buf.at[lax.rem(at, IN_BUFS)], code & 127, (code >> 7) & 31))
        use(group)
        for k in range(GROUP):

            @pl.when(n + k + IN_BUFS < count)
            def _():
                copy(n + k + IN_BUFS).start()

        return carry

    lax.fori_loop(0, (count + GROUP - 1) // GROUP, step, 0)


def add_column(col, alpha):
    def use(group):
        sums = []
        for at, on, tile, own, t in group:
            weight = lane_of(alpha[at // 128], at % 128) * on
            weight = jnp.concatenate([weight] * (BLK // 128), axis=1)
            sums.append(jnp.sum(tile[...] * weight, axis=0, keepdims=True))
        for (at, on, tile, own, t), part in zip(group, sums):
            col[pl.ds(t, 1), :] += part

    return use


def by_slot(table, owns, at):
    return jnp.take_along_axis(table, jnp.broadcast_to(owns[at, pl.ds(0, 1), :], (ROWS, 128)), axis=1)


def first_columns_kernel(slots, owns, potential, m_in, p_ref, col, alpha, buf, sem):
    table = potential[...].T
    for at in range(2):
        alpha[at] = jnp.exp(m_in[at] + by_slot(table, owns, at))
    col[...] = jnp.zeros_like(col)
    stream(slots, p_ref, buf, sem, add_column(col, alpha))


def rows_kernel(slots, weights, alpha, p_ref, row_out, acc, buf, sem):
    acc[...] = jnp.zeros_like(acc)

    def use(group):
        total = jnp.zeros((ROWS, 128), jnp.float32)
        for at, on, tile, own, t in group:
            weight = lane_of(alpha[at // 128], at % 128) * on
            x = tile[...] * weights[pl.ds(t, 1), :]
            x = (x[:, :128] + x[:, 128:256]) + (x[:, 256:384] + x[:, 384:])
            part = jnp.sum(x * weight, axis=1, keepdims=True)
            total = total + jnp.where(lanes() == own, part, 0.0)
        acc[...] += total

    stream(slots, p_ref, buf, sem, use)
    row_out[...] = acc[...].T


def last_columns_kernel(slots, owns, row_sum, alpha, p_ref, col, beta, buf, sem):
    table = row_sum[...].T
    for at in range(2):
        beta[at] = alpha[at] / by_slot(table, owns, at)
    col[...] = jnp.zeros_like(col)
    stream(slots, p_ref, buf, sem, add_column(col, beta))


SMEM = pl.BlockSpec(memory_space=pltpu.SMEM)
VMEM = pl.BlockSpec(memory_space=pltpu.VMEM)
ANY = pl.BlockSpec(memory_space=pl.ANY)


def f32(*shape):
    return jax.ShapeDtypeStruct(shape, jnp.float32)


def call(kernel, ins, outs, out_specs, scratch, limit, aliases={}):
    return pl.pallas_call(
        kernel,
        in_specs=ins,
        out_specs=out_specs,
        out_shape=outs,
        scratch_shapes=scratch,
        input_output_aliases=aliases,
        compiler_params=pltpu.CompilerParams(vmem_limit_bytes=limit * MIB),
    )


def stream_scratch():
    return [pltpu.VMEM((IN_BUFS, ROWS, BLK), jnp.float32), pltpu.SemaphoreType.DMA((IN_BUFS,))]


def padded(rows):
    return jnp.concatenate([rows, jnp.ones((128 - NSRC, ROWS), jnp.float32)], axis=0)


def body(source, target, pairs, live):
    cells, rep = lax.axis_index("cells"), lax.axis_index("rep")
    core, chip = cells % NCORE, cells // NCORE
    at_y, at_z = chip // NZ, chip % NZ
    epsilon = math.sqrt(2.0 * E)

    own_rows = lax.dynamic_index_in_dim(source.reshape(SB, NREP, ROWS, E), rep, 1, False)
    slot = rep * KR + jnp.arange(KR, dtype=jnp.int32)
    note = note_row(jnp.where(slot[None, :] < live[:, None], pairs, -1))
    note = jnp.concatenate(from_reps(note), axis=1).astype(jnp.bfloat16)
    note = jnp.concatenate([note, jnp.zeros((NOTE - 1, E), jnp.bfloat16)])
    early, late = gather_rows(own_rows, note)

    own_targets = target.reshape(TB, BLK, E)
    other_targets = other_core(own_targets)
    wide = own_targets.astype(jnp.float32)
    sq_own = jnp.sum(wide * wide, axis=2) / epsilon
    sq_other = other_core(sq_own)
    sq = jnp.where(
        core == 0, jnp.concatenate([sq_own, sq_other]), jnp.concatenate([sq_other, sq_own])
    )
    wide = own_rows.astype(jnp.float32)
    sq_rows = jnp.sum(wide * wide, axis=2)

    here = jnp.stack([chip, core, at_y, at_z]).astype(jnp.int32)
    scratch = [
        pltpu.VMEM((NY, NZ, SB, ROWS, E), jnp.bfloat16),
        pltpu.VMEM((NTGT, BLK, E), jnp.bfloat16),
        pltpu.VMEM((ROWS, BLK), jnp.float32),
        pltpu.VMEM((ROWS, BLK), jnp.float32),
        pltpu.VMEM((OUT_PAIRS, 2, ROWS, BLK), jnp.float32),
        pltpu.VMEM((NZ, NY, NOTE, E), jnp.bfloat16),
        pltpu.VMEM((NY * NZ, 128), jnp.int32),
        pltpu.SMEM((NY * NZ, 128), jnp.int32),
        pltpu.SemaphoreType.DMA((80,)),
        pltpu.SemaphoreType.DMA((OUT_PAIRS, 2)),
    ]
    state = [
        jax.ShapeDtypeStruct((LIST,), jnp.int32),
        jax.ShapeDtypeStruct((2, 8, 128), jnp.int32),
        f32(NSLOT, ROWS, BLK),
        f32(2, ROWS, 128),
        f32(2, ROWS, 128),
        f32(ROWS, 128),
    ]
    specs = [SMEM, VMEM, ANY, VMEM, VMEM, VMEM]
    first = call(
        functools.partial(tiles_kernel, 2.0 / epsilon, True),
        [SMEM, VMEM, ANY, ANY] + [ANY] * 10,
        state,
        specs,
        scratch,
        40,
    )(here, sq, own_targets, other_targets, *early)
    slots, owns, tiles, tops, _, _, lse = call(
        functools.partial(tiles_kernel, 2.0 / epsilon, False),
        [SMEM, VMEM, ANY, ANY] + [ANY] * 14 + specs,
        state + [f32(128, ROWS)],
        specs + [VMEM],
        scratch,
        40,
        {20: 2},
    )(here, sq, own_targets, other_targets, *early, *late, *first)

    potential = -join_plane(lse[:NSRC], join_lse)

    col, alpha = call(
        first_columns_kernel,
        [SMEM, VMEM, VMEM, VMEM, ANY],
        [f32(NTGT, BLK), f32(2, ROWS, 128)],
        [VMEM, VMEM],
        stream_scratch(),
        24,
    )(slots, owns, padded(potential), tops, tiles)
    col = sum_reps(col + other_core(col))
    weights = 1.0 / (col + math.exp(DUSTBIN))

    row_sum = call(
        rows_kernel,
        [SMEM, VMEM, VMEM, ANY],
        f32(128, ROWS),
        VMEM,
        [pltpu.VMEM((ROWS, 128), jnp.float32)] + stream_scratch(),
        24,
    )(slots, weights, alpha, tiles)
    row_sum = join_plane(row_sum[:NSRC], sum)

    col = call(
        last_columns_kernel,
        [SMEM, VMEM, VMEM, VMEM, ANY],
        f32(NTGT, BLK),
        VMEM,
        [pltpu.VMEM((2, ROWS, 128), jnp.float32)] + stream_scratch(),
        24,
    )(slots, owns, padded(row_sum), alpha, tiles)

    mine = lax.dynamic_slice_in_dim(potential, chip * SB, SB, 0)
    mine = mine - jnp.log(lax.dynamic_slice_in_dim(row_sum, chip * SB, SB, 0))
    f_part = epsilon * mine + sq_rows
    parts = jnp.stack(from_reps(f_part))
    f_out = jnp.stack(
        [lax.dynamic_index_in_dim(parts, (rep - j) % NREP, 0, False) for j in range(NREP)], axis=1
    )

    halves = col.reshape(NCORE, TB, BLK)
    keep = lax.dynamic_index_in_dim(halves, core, 0, False)
    give = lax.dynamic_index_in_dim(halves, 1 - core, 0, False)
    col = sum_reps(keep + other_core(give))
    g_out = -epsilon * jnp.log(col + math.exp(DUSTBIN))
    return f_out.reshape(-1), g_out.reshape(-1)


def solution(mesh):
    in_specs = (P("cells", None), P("cells", None), P("cells", "rep"), P("cells"))
    out_specs = (P("cells"), P("cells"))
    return jax.shard_map(body, mesh=mesh, in_specs=in_specs, out_specs=out_specs, check_vma=False)
```

```python
import functools
import math

import jax
import jax.numpy as jnp
from jax import lax
from jax.experimental import pallas as pl
from jax.experimental.pallas import tpu as pltpu
from jax.sharding import PartitionSpec as P

DUSTBIN = -1.0
LOWEST = -1e30

NY, NZ, NCORE, NREP = 4, 8, 2, 4
SB, TB, KR, BLK, E = 3, 16, 8, 512, 256
ROWS = BLK // NREP
A_ROWS, B_ROWS = 64, 64
NSRC = NY * NZ * SB
NTGT = NCORE * TB
NSLOT = NY * NZ * NREP * NCORE
AT_COUNT, LIST = NSLOT, NSLOT + 128
IN_BUFS, OUT_BUFS, GROUP = 32, 8, 4
NOTE = 16
MIB = 1 << 20
NEAR_Y, NEAR_Z = (0, 1, 3), (0, 1, 2, 3, 5, 6, 7)


def cell(y, z, core):
    return ((y % NY) * NZ + z % NZ) * NCORE + core


def plane_shift(a, dy, dz):
    perm = [
        (cell(y, z, c), cell(y + dy, z + dz, c))
        for y in range(NY) for z in range(NZ) for c in range(NCORE)
    ]
    return lax.ppermute(a, "cells", perm)


def other_core(a):
    return lax.ppermute(a, "cells", [(i, i ^ 1) for i in range(NY * NZ * NCORE)])


def rep_shift(a, k):
    return lax.ppermute(a, "rep", [(i, (i + k) % NREP) for i in range(NREP)])


def from_reps(a):
    return [a] + [rep_shift(a, k) for k in range(1, NREP)]


def sum_reps(a):
    p = from_reps(a)
    return (p[0] + p[2]) + (p[1] + p[3])


def join_plane(a, join):
    a = join([a] + [plane_shift(a, k, 0) for k in range(1, NY)])
    a = join([a, plane_shift(a, 0, 1)])
    return join([a] + [plane_shift(a, 0, k) for k in range(2, NZ, 2)])


def join_lse(parts):
    top = functools.reduce(jnp.maximum, parts)
    return top + jnp.log(sum(jnp.exp(p - top) for p in parts))


def gather_rows(xs, note):
    a = xs[:, :A_ROWS].reshape(SB * A_ROWS, E)
    b = jnp.concatenate([xs[:, A_ROWS:].reshape(SB * B_ROWS, E), note])
    up1, down1 = plane_shift(a, 0, 1), plane_shift(a, 0, -1)
    up2, down2 = plane_shift(a, 0, 2), plane_shift(a, 0, -2)
    up3, down3, up4 = plane_shift(up2, 0, 1), plane_shift(down2, 0, -1), plane_shift(up2, 0, 2)
    zcat = jnp.stack([a, up1, up2, up3, up4, down3, down2, down1])
    ycat = jnp.stack([b, plane_shift(b, 1, 0), plane_shift(b, 2, 0), plane_shift(b, 3, 0)])
    y1, y3 = plane_shift(zcat, 1, 0), plane_shift(zcat, -1, 0)
    z1, z7 = plane_shift(ycat, 0, 1), plane_shift(ycat, 0, -1)
    z2, z6 = plane_shift(z1, 0, 1), plane_shift(z7, 0, -1)
    z3, z5 = plane_shift(z2, 0, 1), plane_shift(z6, 0, -1)
    y2a, y2b = plane_shift(y1[:4], 1, 0), plane_shift(y3[4:], -1, 0)
    z4a, z4b = plane_shift(z3[:2], 0, 1), plane_shift(z5[2:], 0, -1)
    return [zcat, y1, y3, ycat, z1, z2, z3, z5, z6, z7, y2a, y2b, z4a, z4b]


def pieces(xs, xbuf):
    out = []

    def put(src, dy, dz, second):
        rows, count = (pl.ds(A_ROWS, B_ROWS), B_ROWS) if second else (pl.ds(0, A_ROWS), A_ROWS)
        for block in range(SB):
            out.append((src.at[:, pl.ds(block * count, count)], xbuf.at[dy, dz, block, rows]))

    for src, dy in zip(xs[:3], NEAR_Y):
        put(src, dy, slice(None), False)
    for src, dz in zip(xs[3:10], NEAR_Z):
        put(src, slice(None), dz, True)
    put(xs[10], 2, pl.ds(0, 4), False)
    put(xs[11], 2, pl.ds(4, 4), False)
    put(xs[12], pl.ds(0, 2), 4, True)
    put(xs[13], pl.ds(2, 2), 4, True)
    return out


def note_row(masked):
    named = masked.reshape(SB * KR, 1)
    block = (jnp.arange(SB * KR, dtype=jnp.int32) // KR)[:, None]
    owner = jnp.arange(NY * NZ * NCORE, dtype=jnp.int32)[None, :]
    hit = (named >= owner * TB) & (named < (owner + 1) * TB)
    return jnp.sum(jnp.where(hit, 1 + TB * block + named - owner * TB, 0), axis=0, keepdims=True)


def lanes():
    return lax.broadcasted_iota(jnp.int32, (ROWS, 128), 1)


def lane_of(a, at):
    return jnp.take_along_axis(a, jnp.full((ROWS, 128), at, jnp.int32), axis=1)


def tiles_kernel(scale, here, sq, y_own, y_other, *refs):
    xs, refs = refs[:14], refs[14:]
    slots, owns, p_out, m_out, lse_out, l_out, top = refs[:7]
    xbuf, ybuf, even, odd, pbuf, mbuf, found, found_s, sem, p_sem = refs[7:]
    chip, core, at_y, at_z = here[0], here[1], here[2], here[3]

    note_copies = []
    for x, dz in zip(xs[3:10], NEAR_Z):
        note_copies.append((x.at[:, pl.ds(SB * B_ROWS, NOTE)], mbuf.at[dz]))
    for x, dy in zip(xs[12:], (0, 2)):
        note_copies.append((x.at[:, pl.ds(SB * B_ROWS, NOTE)], mbuf.at[4, pl.ds(dy, 2)]))
    note_copies = [
        pltpu.make_async_copy(src, dst, sem.at[i]) for i, (src, dst) in enumerate(note_copies)
    ]
    copies = [
        pltpu.make_async_copy(y_own, ybuf.at[pl.ds(core * TB, TB)], sem.at[10]),
        pltpu.make_async_copy(y_other, ybuf.at[pl.ds((1 - core) * TB, TB)], sem.at[11]),
    ]
    parts = pieces(xs, xbuf)
    for i, (src, dst) in enumerate(parts):
        copies.append(pltpu.make_async_copy(src, dst, sem.at[12 + i]))
    at = 12 + len(parts)
    for copy in note_copies + copies:
        copy.start()
    top[...] = jnp.full_like(top, LOWEST)
    m_out[...] = jnp.zeros_like(m_out)
    l_out[...] = jnp.zeros_like(l_out)
    owns[...] = jnp.zeros_like(owns)
    for copy in note_copies:
        copy.wait()

    source_lane = lax.broadcasted_iota(jnp.int32, (E, 128), 0)
    lane = lax.broadcasted_iota(jnp.int32, (E, 128), 1)
    wanted = (lane < NREP * NCORE) & (
        source_lane == (lane >> 1) * (NY * NZ * NCORE) + chip * NCORE + (lane & 1)
    )
    picked = lax.dot_general(
        mbuf[...].reshape(NY * NZ * NOTE, E), wanted.astype(jnp.bfloat16), (((1,), (0,)), ((), ())),
        preferred_element_type=jnp.float32,
    )
    found[...] = picked.reshape(NY * NZ, NOTE, 128)[:, 0].astype(jnp.int32)
    move = pltpu.make_async_copy(found, found_s, sem.at[at])
    move.start()
    move.wait()

    def of_chip(dz, dy, n):
        base = (((at_y - dy) & (NY - 1)) * NZ + ((at_z - dz) & (NZ - 1))) * SB
        where = (dy << 5) | (dz << 2)
        for j in range(NREP * NCORE):
            value = found_s[dz * NY + dy, j] - 1
            block = value >> 4
            t = (value & (TB - 1)) + (j & 1) * TB
            slots[n] = ((where | block) << 12) | (t << 7) | (base + block)
            n = n + (value >= 0).astype(jnp.int32)
        return n

    named = jnp.int32(0)
    for dz in range(NZ):
        for dy in range(NY):
            named = of_chip(dz, dy, named)
    count = (named + 3) & ~3
    for k in range(3):
        slots[named + k] = slots[jnp.maximum(named - 1, 0)]
    slots[AT_COUNT] = count
    for copy in copies:
        copy.wait()

    def score(n, into):
        code = slots[jnp.minimum(n, count - 1)]
        t, block, dz, dy = (code >> 7) & 31, (code >> 12) & 3, (code >> 14) & 7, (code >> 17) & 3
        inner = lax.dot_general(
            xbuf[dy, dz, block], ybuf[t],
            (((1,), (1,)), ((), ())), preferred_element_type=jnp.float32,
        )
        into[...] = inner - sq[pl.ds(t, 1), :]

    def out_copies(n, ring):
        return pltpu.make_async_copy(pbuf.at[ring], p_out.at[pl.ds(n, 2)], p_sem.at[ring])

    def pair(n, now, later):
        done = n // 2
        ring = lax.rem(done, OUT_BUFS)

        @pl.when(done >= OUT_BUFS)
        def _():
            out_copies(n - 2 * OUT_BUFS, ring).wait()

        highs, parts = [], []
        for k in range(2):
            score(n + 2 + k, later[k])
            values = now[k][...]
            high = jnp.max(values, axis=1, keepdims=True)
            weight = jnp.exp2((values - high) * (scale * math.log2(math.e)))
            pbuf[ring, k] = weight
            highs.append(high * scale)
            parts.append(jnp.sum(weight, axis=1, keepdims=True))
        half, lane = n // 128, lanes()
        m, total, most, own_of = m_out[half], l_out[half], top[...], owns[half]
        for k in range(2):
            own, mine = slots[n + k] & 127, lane == (n + k) % 128
            m = jnp.where(mine, jnp.where(n + k < named, highs[k], LOWEST), m)
            total = jnp.where(mine, jnp.where(n + k < named, parts[k], 0.0), total)
            own_of = jnp.where(mine[:8], own, own_of)
            most = jnp.where(lane == own, jnp.maximum(most, highs[k]), most)
        m_out[half], l_out[half], top[...], owns[half] = m, total, most, own_of
        out_copies(n, ring).start()

    evens, odds = (even.at[0], even.at[1]), (odd.at[0], odd.at[1])

    @pl.when(count > 0)
    def _():
        for k in range(2):
            score(k, evens[k])

    def step(i, carry):
        n = 4 * i
        pair(n, evens, odds)
        pair(n + 2, odds, evens)
        return carry

    lax.fori_loop(0, count // 4, step, 0)

    def drain(done, carry):
        out_copies(2 * done, lax.rem(done, OUT_BUFS)).wait()
        return carry

    pairs = count // 2
    lax.fori_loop(jnp.maximum(pairs - OUT_BUFS, 0), pairs, drain, 0)
    total = jnp.zeros((ROWS, 128), jnp.float32)
    for half in range(2):
        scaled = l_out[half] * jnp.exp(m_out[half] - by_slot(top[...], owns, half))
        own_rows = lax.broadcasted_iota(jnp.int32, (128, 128), 0)
        one_hot = (own_rows == owns[half, pl.ds(0, 1), :]).astype(jnp.float32)
        total = total + lax.dot_general(
            jnp.where(l_out[half] > 0.0, scaled, 0.0), one_hot, (((1,), (1,)), ((), ())),
            precision=lax.Precision.HIGHEST, preferred_element_type=jnp.float32,
        )
    some = total > 0.0
    lse = jnp.where(some, top[...] + jnp.log(jnp.where(some, total, 1.0)), LOWEST)
    lse_out[...] = lse.T


def stream(slots, p_ref, buf, sem, use):
    count = slots[AT_COUNT]

    def copy(n):
        at = lax.rem(n, IN_BUFS)
        return pltpu.make_async_copy(p_ref.at[n], buf.at[at], sem.at[at])

    def start(n, carry):
        copy(n).start()
        return carry

    lax.fori_loop(0, jnp.minimum(count, IN_BUFS), start, 0)

    def step(i, carry):
        n = i * GROUP
        group = []
        for k in range(GROUP):
            copy(n + k).wait()
            code = slots[n + k]
            group.append((n + k, buf.at[lax.rem(n + k, IN_BUFS)], code & 127, (code >> 7) & 31))
        use(group)

        @pl.when(n + IN_BUFS < count)
        def _():
            for k in range(GROUP):
                copy(n + k + IN_BUFS).start()

        return carry

    lax.fori_loop(0, count // GROUP, step, 0)


def add_column(col, alpha):
    def use(group):
        sums = []
        for at, tile, own, t in group:
            weight = lane_of(alpha[at // 128], at % 128)
            weight = jnp.concatenate([weight] * (BLK // 128), axis=1)
            sums.append(jnp.sum(tile[...] * weight, axis=0, keepdims=True))
        for (at, tile, own, t), part in zip(group, sums):
            col[pl.ds(t, 1), :] += part

    return use


def by_slot(table, owns, at):
    return jnp.take_along_axis(table, jnp.broadcast_to(owns[at, pl.ds(0, 1), :], (ROWS, 128)), axis=1)


def first_columns_kernel(slots, owns, potential, m_in, p_ref, col, alpha, buf, sem):
    table = potential[...].T
    for at in range(2):
        alpha[at] = jnp.exp(m_in[at] + by_slot(table, owns, at))
    col[...] = jnp.zeros_like(col)
    stream(slots, p_ref, buf, sem, add_column(col, alpha))


def rows_kernel(slots, weights, alpha, p_ref, row_out, acc, buf, sem):
    acc[...] = jnp.zeros_like(acc)

    def use(group):
        total = jnp.zeros((ROWS, 128), jnp.float32)
        for at, tile, own, t in group:
            weight = lane_of(alpha[at // 128], at % 128)
            x = tile[...] * weights[pl.ds(t, 1), :]
            x = (x[:, :128] + x[:, 128:256]) + (x[:, 256:384] + x[:, 384:])
            part = jnp.sum(x * weight, axis=1, keepdims=True)
            total = total + jnp.where(lanes() == own, part, 0.0)
        acc[...] += total

    stream(slots, p_ref, buf, sem, use)
    row_out[...] = acc[...].T


def last_columns_kernel(slots, owns, row_sum, alpha, p_ref, col, beta, buf, sem):
    table = row_sum[...].T
    for at in range(2):
        beta[at] = alpha[at] / by_slot(table, owns, at)
    col[...] = jnp.zeros_like(col)
    stream(slots, p_ref, buf, sem, add_column(col, beta))


SMEM = pl.BlockSpec(memory_space=pltpu.SMEM)
VMEM = pl.BlockSpec(memory_space=pltpu.VMEM)
ANY = pl.BlockSpec(memory_space=pl.ANY)


def f32(*shape):
    return jax.ShapeDtypeStruct(shape, jnp.float32)


def call(kernel, ins, outs, out_specs, scratch, limit, aliases={}, cost=24 << 20):
    return pl.pallas_call(
        kernel,
        in_specs=ins,
        out_specs=out_specs,
        out_shape=outs,
        scratch_shapes=scratch,
        input_output_aliases=aliases,
        cost_estimate=pl.CostEstimate(flops=0, bytes_accessed=cost, transcendentals=0),
        compiler_params=pltpu.CompilerParams(vmem_limit_bytes=limit * MIB),
    )


def stream_scratch():
    return [pltpu.VMEM((IN_BUFS, ROWS, BLK), jnp.float32), pltpu.SemaphoreType.DMA((IN_BUFS,))]


def padded(rows):
    return jnp.concatenate([rows, jnp.ones((128 - NSRC, ROWS), jnp.float32)], axis=0)


def body(source, target, pairs, live):
    cells, rep = lax.axis_index("cells"), lax.axis_index("rep")
    core, chip = cells % NCORE, cells // NCORE
    at_y, at_z = chip // NZ, chip % NZ
    epsilon = math.sqrt(2.0 * E)

    own_rows = lax.dynamic_index_in_dim(source.reshape(SB, NREP, ROWS, E), rep, 1, False)
    slot = rep * KR + jnp.arange(KR, dtype=jnp.int32)
    note = note_row(jnp.where(slot[None, :] < live[:, None], pairs, -1))
    note = jnp.concatenate(from_reps(note), axis=1).astype(jnp.bfloat16)
    note = jnp.concatenate([note, jnp.zeros((NOTE - 1, E), jnp.bfloat16)])
    gathered = gather_rows(own_rows, note)

    own_targets = target.reshape(TB, BLK, E)
    other_targets = other_core(own_targets)
    wide = own_targets.astype(jnp.float32)
    sq_own = jnp.sum(wide * wide, axis=2) * 0.5
    sq_other = other_core(sq_own)
    sq = jnp.where(
        core == 0, jnp.concatenate([sq_own, sq_other]), jnp.concatenate([sq_other, sq_own])
    )
    wide = own_rows.astype(jnp.float32)
    sq_rows = jnp.sum(wide * wide, axis=2)

    here = jnp.stack([chip, core, at_y, at_z]).astype(jnp.int32)
    scratch = [
        pltpu.VMEM((NY, NZ, SB, ROWS, E), jnp.bfloat16),
        pltpu.VMEM((NTGT, BLK, E), jnp.bfloat16),
        pltpu.VMEM((2, ROWS, BLK), jnp.float32),
        pltpu.VMEM((2, ROWS, BLK), jnp.float32),
        pltpu.VMEM((OUT_BUFS, 2, ROWS, BLK), jnp.float32),
        pltpu.VMEM((NZ, NY, NOTE, E), jnp.bfloat16),
        pltpu.VMEM((NY * NZ, 128), jnp.int32),
        pltpu.SMEM((NY * NZ, 128), jnp.int32),
        pltpu.SemaphoreType.DMA((64,)),
        pltpu.SemaphoreType.DMA((OUT_BUFS,)),
    ]
    slots, owns, tiles, tops, lse = call(
        functools.partial(tiles_kernel, 2.0 / epsilon),
        [SMEM, VMEM, ANY, ANY] + [ANY] * 14,
        [
            jax.ShapeDtypeStruct((LIST,), jnp.int32),
            jax.ShapeDtypeStruct((2, 8, 128), jnp.int32),
            f32(NSLOT, ROWS, BLK),
            f32(2, ROWS, 128),
            f32(128, ROWS),
        ],
        [SMEM, VMEM, ANY, VMEM, VMEM],
        [pltpu.VMEM((2, ROWS, 128), jnp.float32), pltpu.VMEM((ROWS, 128), jnp.float32)] + scratch,
        60,
    )(here, sq, own_targets, other_targets, *gathered)

    potential = -join_plane(lse[:NSRC], join_lse)

    col, alpha = call(
        first_columns_kernel,
        [SMEM, VMEM, VMEM, VMEM, ANY],
        [f32(NTGT, BLK), f32(2, ROWS, 128)],
        [VMEM, VMEM],
        stream_scratch(),
        24,
    )(slots, owns, padded(potential), tops, tiles)
    col = sum_reps(col + other_core(col))
    weights = 1.0 / (col + math.exp(DUSTBIN))

    row_sum = call(
        rows_kernel,
        [SMEM, VMEM, VMEM, ANY],
        f32(128, ROWS),
        VMEM,
        [pltpu.VMEM((ROWS, 128), jnp.float32)] + stream_scratch(),
        24,
    )(slots, weights, alpha, tiles)
    row_sum = join_plane(row_sum[:NSRC], sum)

    col = call(
        last_columns_kernel,
        [SMEM, VMEM, VMEM, VMEM, ANY],
        f32(NTGT, BLK),
        VMEM,
        [pltpu.VMEM((2, ROWS, 128), jnp.float32)] + stream_scratch(),
        24,
    )(slots, owns, padded(row_sum), alpha, tiles)

    mine = lax.dynamic_slice_in_dim(potential, chip * SB, SB, 0)
    mine = mine - jnp.log(lax.dynamic_slice_in_dim(row_sum, chip * SB, SB, 0))
    f_part = epsilon * mine + sq_rows
    parts = jnp.stack(from_reps(f_part))
    f_out = jnp.stack(
        [lax.dynamic_index_in_dim(parts, (rep - j) % NREP, 0, False) for j in range(NREP)], axis=1
    )

    halves = col.reshape(NCORE, TB, BLK)
    keep = lax.dynamic_index_in_dim(halves, core, 0, False)
    give = lax.dynamic_index_in_dim(halves, 1 - core, 0, False)
    col = sum_reps(keep + other_core(give))
    g_out = -epsilon * jnp.log(col + math.exp(DUSTBIN))
    return f_out.reshape(-1), g_out.reshape(-1)


def solution(mesh):
    in_specs = (P("cells", None), P("cells", None), P("cells", "rep"), P("cells"))
    out_specs = (P("cells"), P("cells"))
    return jax.shard_map(body, mesh=mesh, in_specs=in_specs, out_specs=out_specs, check_vma=False)
```

```python
import functools
import math

import jax
import jax.numpy as jnp
from jax import lax
from jax.experimental import pallas as pl
from jax.experimental.pallas import tpu as pltpu
from jax.sharding import PartitionSpec as P

DUSTBIN = -1.0
LOWEST = -1e30

NY, NZ, NCORE, NREP = 4, 8, 2, 4
SB, TB, KR, BLK, E = 3, 16, 8, 512, 256
ROWS = BLK // NREP
A_ROWS, B_ROWS = 64, 64
NSRC = NY * NZ * SB
NTGT = NCORE * TB
NSLOT = NY * NZ * NREP * NCORE
AT_COUNT, LIST = NSLOT, NSLOT + 128
IN_BUFS, OUT_BUFS, GROUP = 32, 8, 4
NOTE = 16
MIB = 1 << 20
NEAR_Y, NEAR_Z = (0, 1, 3), (0, 1, 2, 3, 5, 6, 7)


def cell(y, z, core):
    return ((y % NY) * NZ + z % NZ) * NCORE + core


def plane_shift(a, dy, dz):
    perm = [
        (cell(y, z, c), cell(y + dy, z + dz, c))
        for y in range(NY) for z in range(NZ) for c in range(NCORE)
    ]
    return lax.ppermute(a, "cells", perm)


def other_core(a):
    return lax.ppermute(a, "cells", [(i, i ^ 1) for i in range(NY * NZ * NCORE)])


def rep_shift(a, k):
    return lax.ppermute(a, "rep", [(i, (i + k) % NREP) for i in range(NREP)])


def from_reps(a):
    return [a] + [rep_shift(a, k) for k in range(1, NREP)]


def sum_four(p):
    return (p[0] + p[2]) + (p[1] + p[3])


def join_plane(a, join):
    a = join([a] + [plane_shift(a, k, 0) for k in range(1, NY)])
    a = join([a, plane_shift(a, 0, 1)])
    return [a] + [plane_shift(a, 0, k) for k in range(2, NZ, 2)]


def join_lse(parts):
    top = functools.reduce(jnp.maximum, parts)
    return top + jnp.log(sum(jnp.exp(p - top) for p in parts))


def gather_rows(xs, note):
    a = xs[:, :A_ROWS].reshape(SB * A_ROWS, E)
    b = jnp.concatenate([xs[:, A_ROWS:].reshape(SB * B_ROWS, E), note])
    up1, down1 = plane_shift(a, 0, 1), plane_shift(a, 0, -1)
    up2, down2 = plane_shift(a, 0, 2), plane_shift(a, 0, -2)
    up3, down3, up4 = plane_shift(up2, 0, 1), plane_shift(down2, 0, -1), plane_shift(up2, 0, 2)
    zcat = jnp.stack([a, up1, up2, up3, up4, down3, down2, down1])
    ycat = jnp.stack([b, plane_shift(b, 1, 0), plane_shift(b, 2, 0), plane_shift(b, 3, 0)])
    y1, y3 = plane_shift(zcat, 1, 0), plane_shift(zcat, -1, 0)
    z1, z7 = plane_shift(ycat, 0, 1), plane_shift(ycat, 0, -1)
    z2, z6 = plane_shift(z1, 0, 1), plane_shift(z7, 0, -1)
    z3, z5 = plane_shift(z2, 0, 1), plane_shift(z6, 0, -1)
    y2a, y2b = plane_shift(y1[:4], 1, 0), plane_shift(y3[4:], -1, 0)
    z4a, z4b = plane_shift(z3[:2], 0, 1), plane_shift(z5[2:], 0, -1)
    return [zcat, y1, y3, ycat, z1, z2, z3, z5, z6, z7, y2a, y2b, z4a, z4b]


def pieces(xs, xbuf):
    out = []

    def put(src, dy, dz, second):
        rows, count = (pl.ds(A_ROWS, B_ROWS), B_ROWS) if second else (pl.ds(0, A_ROWS), A_ROWS)
        for block in range(SB):
            out.append((src.at[:, pl.ds(block * count, count)], xbuf.at[dy, dz, block, rows]))

    for src, dy in zip(xs[:3], NEAR_Y):
        put(src, dy, slice(None), False)
    for src, dz in zip(xs[3:10], NEAR_Z):
        put(src, slice(None), dz, True)
    put(xs[10], 2, pl.ds(0, 4), False)
    put(xs[11], 2, pl.ds(4, 4), False)
    put(xs[12], pl.ds(0, 2), 4, True)
    put(xs[13], pl.ds(2, 2), 4, True)
    return out


def note_row(masked):
    named = masked.reshape(SB * KR, 1)
    block = (jnp.arange(SB * KR, dtype=jnp.int32) // KR)[:, None]
    owner = jnp.arange(NY * NZ * NCORE, dtype=jnp.int32)[None, :]
    hit = (named >= owner * TB) & (named < (owner + 1) * TB)
    return jnp.sum(jnp.where(hit, 1 + TB * block + named - owner * TB, 0), axis=0, keepdims=True)


def lanes():
    return lax.broadcasted_iota(jnp.int32, (ROWS, 128), 1)


def lane_of(a, at):
    return jnp.take_along_axis(a, jnp.full((ROWS, 128), at, jnp.int32), axis=1)


def tiles_kernel(scale, here, sq, y_own, y_other, *refs):
    xs, refs = refs[:14], refs[14:]
    slots, owns, p_out, m_out, lse_out, l_out, top = refs[:7]
    xbuf, ybuf, even, odd, pbuf, mbuf, found, found_s, sem, p_sem = refs[7:]
    chip, core, at_y, at_z = here[0], here[1], here[2], here[3]

    note_copies = []
    for x, dz in zip(xs[3:10], NEAR_Z):
        note_copies.append((x.at[:, pl.ds(SB * B_ROWS, NOTE)], mbuf.at[dz]))
    for x, dy in zip(xs[12:], (0, 2)):
        note_copies.append((x.at[:, pl.ds(SB * B_ROWS, NOTE)], mbuf.at[4, pl.ds(dy, 2)]))
    note_copies = [
        pltpu.make_async_copy(src, dst, sem.at[i]) for i, (src, dst) in enumerate(note_copies)
    ]
    copies = [
        pltpu.make_async_copy(y_own, ybuf.at[pl.ds(core * TB, TB)], sem.at[10]),
        pltpu.make_async_copy(y_other, ybuf.at[pl.ds((1 - core) * TB, TB)], sem.at[11]),
    ]
    parts = pieces(xs, xbuf)
    for i, (src, dst) in enumerate(parts):
        copies.append(pltpu.make_async_copy(src, dst, sem.at[12 + i]))
    at = 12 + len(parts)
    for copy in note_copies + copies:
        copy.start()
    top[...] = jnp.full_like(top, LOWEST)
    m_out[...] = jnp.zeros_like(m_out)
    l_out[...] = jnp.zeros_like(l_out)
    owns[...] = jnp.zeros_like(owns)
    for copy in note_copies:
        copy.wait()

    source_lane = lax.broadcasted_iota(jnp.int32, (E, 128), 0)
    lane = lax.broadcasted_iota(jnp.int32, (E, 128), 1)
    wanted = (lane < NREP * NCORE) & (
        source_lane == (lane >> 1) * (NY * NZ * NCORE) + chip * NCORE + (lane & 1)
    )
    picked = lax.dot_general(
        mbuf[...].reshape(NY * NZ * NOTE, E), wanted.astype(jnp.bfloat16), (((1,), (0,)), ((), ())),
        preferred_element_type=jnp.float32,
    )
    found[...] = picked.reshape(NY * NZ, NOTE, 128)[:, 0].astype(jnp.int32)
    move = pltpu.make_async_copy(found, found_s, sem.at[at])
    move.start()
    move.wait()

    def of_chip(dz, dy, n):
        base = (((at_y - dy) & (NY - 1)) * NZ + ((at_z - dz) & (NZ - 1))) * SB
        where = (dy << 5) | (dz << 2)
        for j in range(NREP * NCORE):
            value = found_s[dz * NY + dy, j] - 1
            block = value >> 4
            t = (value & (TB - 1)) + (j & 1) * TB
            slots[n] = ((where | block) << 12) | (t << 7) | (base + block)
            n = n + (value >= 0).astype(jnp.int32)
        return n

    named = jnp.int32(0)
    for dz in range(NZ):
        for dy in range(NY):
            named = of_chip(dz, dy, named)
    count = (named + 3) & ~3
    for k in range(3):
        slots[named + k] = slots[jnp.maximum(named - 1, 0)]
    slots[AT_COUNT] = count
    for copy in copies:
        copy.wait()

    def score(n, into):
        code = slots[jnp.minimum(n, count - 1)]
        t, block, dz, dy = (code >> 7) & 31, (code >> 12) & 3, (code >> 14) & 7, (code >> 17) & 3
        inner = lax.dot_general(
            xbuf[dy, dz, block], ybuf[t],
            (((1,), (1,)), ((), ())), preferred_element_type=jnp.float32,
        )
        into[...] = inner - sq[pl.ds(t, 1), :]

    def out_copies(n, ring):
        return pltpu.make_async_copy(pbuf.at[ring], p_out.at[pl.ds(n, 2)], p_sem.at[ring])

    def pair(n, now, later):
        done = n // 2
        ring = lax.rem(done, OUT_BUFS)

        @pl.when(done >= OUT_BUFS)
        def _():
            out_copies(n - 2 * OUT_BUFS, ring).wait()

        highs, parts = [], []
        for k in range(2):
            score(n + 2 + k, later[k])
            values = now[k][...]
            high = jnp.max(values, axis=1, keepdims=True)
            weight = jnp.exp2((values - high) * (scale * math.log2(math.e)))
            pbuf[ring, k] = weight
            highs.append(high * scale)
            parts.append(jnp.sum(weight, axis=1, keepdims=True))
        half, lane = n // 128, lanes()
        m, total, most, own_of = m_out[half], l_out[half], top[...], owns[half]
        for k in range(2):
            own, mine = slots[n + k] & 127, lane == (n + k) % 128
            m = jnp.where(mine, jnp.where(n + k < named, highs[k], LOWEST), m)
            total = jnp.where(mine, jnp.where(n + k < named, parts[k], 0.0), total)
            own_of = jnp.where(mine[:8], own, own_of)
            most = jnp.where(lane == own, jnp.maximum(most, highs[k]), most)
        m_out[half], l_out[half], top[...], owns[half] = m, total, most, own_of
        out_copies(n, ring).start()

    evens, odds = (even.at[0], even.at[1]), (odd.at[0], odd.at[1])

    @pl.when(count > 0)
    def _():
        for k in range(2):
            score(k, evens[k])

    def step(i, carry):
        n = 4 * i
        pair(n, evens, odds)
        pair(n + 2, odds, evens)
        return carry

    lax.fori_loop(0, count // 4, step, 0)

    def drain(done, carry):
        out_copies(2 * done, lax.rem(done, OUT_BUFS)).wait()
        return carry

    pairs = count // 2
    lax.fori_loop(jnp.maximum(pairs - OUT_BUFS, 0), pairs, drain, 0)
    total = jnp.zeros((ROWS, 128), jnp.float32)
    for half in range(2):
        scaled = l_out[half] * jnp.exp(m_out[half] - by_slot(top[...], owns, half))
        own_rows = lax.broadcasted_iota(jnp.int32, (128, 128), 0)
        one_hot = (own_rows == owns[half, pl.ds(0, 1), :]).astype(jnp.float32)
        total = total + lax.dot_general(
            jnp.where(l_out[half] > 0.0, scaled, 0.0), one_hot, (((1,), (1,)), ((), ())),
            precision=lax.Precision.HIGHEST, preferred_element_type=jnp.float32,
        )
    some = total > 0.0
    lse = jnp.where(some, top[...] + jnp.log(jnp.where(some, total, 1.0)), LOWEST)
    lse_out[...] = lse.T[:NSRC]


def tile_copy(slots, p_ref, buf, sem):
    def copy(n):
        at = lax.rem(n, IN_BUFS)
        return pltpu.make_async_copy(p_ref.at[n], buf.at[at], sem.at[at])

    def start(n, carry):
        copy(n).start()
        return carry

    lax.fori_loop(0, jnp.minimum(slots[AT_COUNT], IN_BUFS), start, 0)
    return copy


def stream(slots, copy, buf, use):
    count = slots[AT_COUNT]

    def step(i, carry):
        n = i * GROUP
        group = []
        for k in range(GROUP):
            copy(n + k).wait()
            code = slots[n + k]
            group.append((n + k, buf.at[lax.rem(n + k, IN_BUFS)], code & 127, (code >> 7) & 31))
        use(group)

        @pl.when(n + IN_BUFS < count)
        def _():
            for k in range(GROUP):
                copy(n + k + IN_BUFS).start()

        return carry

    lax.fori_loop(0, count // GROUP, step, 0)


def add_column(col, alpha):
    def use(group):
        sums = []
        for at, tile, own, t in group:
            weight = lane_of(alpha[at // 128], at % 128)
            weight = jnp.concatenate([weight] * (BLK // 128), axis=1)
            sums.append(jnp.sum(tile[...] * weight, axis=0, keepdims=True))
        for (at, tile, own, t), part in zip(group, sums):
            col[pl.ds(t, 1), :] += part

    return use


def by_slot(table, owns, at):
    return jnp.take_along_axis(table, jnp.broadcast_to(owns[at, pl.ds(0, 1), :], (ROWS, 128)), axis=1)


def by_lane(rows):
    return jnp.concatenate([rows[...], jnp.ones((128 - NSRC, ROWS), jnp.float32)], axis=0).T


def first_columns_kernel(slots, owns, *refs):
    parts, (m_in, p_ref, col, alpha, potential, buf, sem) = refs[:4], refs[4:]
    copy = tile_copy(slots, p_ref, buf, sem)
    potential[...] = -join_lse([part[...] for part in parts])
    table = by_lane(potential)
    for at in range(2):
        alpha[at] = jnp.exp(m_in[at] + by_slot(table, owns, at))
    col[...] = jnp.zeros_like(col)
    stream(slots, copy, buf, add_column(col, alpha))


def rows_kernel(slots, *refs):
    parts, (alpha, p_ref, row_out, weights, acc, buf, sem) = refs[:4], refs[4:]
    copy = tile_copy(slots, p_ref, buf, sem)
    weights[...] = 1.0 / (sum_four([part[...] for part in parts]) + math.exp(DUSTBIN))
    acc[...] = jnp.zeros_like(acc)

    def use(group):
        total = jnp.zeros((ROWS, 128), jnp.float32)
        for at, tile, own, t in group:
            weight = lane_of(alpha[at // 128], at % 128)
            x = tile[...] * weights[pl.ds(t, 1), :]
            x = (x[:, :128] + x[:, 128:256]) + (x[:, 256:384] + x[:, 384:])
            part = jnp.sum(x * weight, axis=1, keepdims=True)
            total = total + jnp.where(lanes() == own, part, 0.0)
        acc[...] += total

    stream(slots, copy, buf, use)
    row_out[...] = acc[...].T[:NSRC]


def last_columns_kernel(slots, owns, row_sum, alpha, p_ref, col, beta, buf, sem):
    copy = tile_copy(slots, p_ref, buf, sem)
    table = by_lane(row_sum)
    for at in range(2):
        beta[at] = alpha[at] / by_slot(table, owns, at)
    col[...] = jnp.zeros_like(col)
    stream(slots, copy, buf, add_column(col, beta))


SMEM = pl.BlockSpec(memory_space=pltpu.SMEM)
VMEM = pl.BlockSpec(memory_space=pltpu.VMEM)
ANY = pl.BlockSpec(memory_space=pl.ANY)


def f32(*shape):
    return jax.ShapeDtypeStruct(shape, jnp.float32)


def call(kernel, ins, outs, out_specs, scratch, limit, aliases={}, cost=24 << 20):
    return pl.pallas_call(
        kernel,
        in_specs=ins,
        out_specs=out_specs,
        out_shape=outs,
        scratch_shapes=scratch,
        input_output_aliases=aliases,
        cost_estimate=pl.CostEstimate(flops=0, bytes_accessed=cost, transcendentals=0),
        compiler_params=pltpu.CompilerParams(vmem_limit_bytes=limit * MIB),
    )


def stream_scratch():
    return [pltpu.VMEM((IN_BUFS, ROWS, BLK), jnp.float32), pltpu.SemaphoreType.DMA((IN_BUFS,))]


def body(source, target, pairs, live):
    cells, rep = lax.axis_index("cells"), lax.axis_index("rep")
    core, chip = cells % NCORE, cells // NCORE
    at_y, at_z = chip // NZ, chip % NZ
    epsilon = math.sqrt(2.0 * E)

    own_rows = lax.dynamic_index_in_dim(source.reshape(SB, NREP, ROWS, E), rep, 1, False)
    slot = rep * KR + jnp.arange(KR, dtype=jnp.int32)
    note = note_row(jnp.where(slot[None, :] < live[:, None], pairs, -1))
    note = jnp.concatenate(from_reps(note), axis=1).astype(jnp.bfloat16)
    note = jnp.concatenate([note, jnp.zeros((NOTE - 1, E), jnp.bfloat16)])
    gathered = gather_rows(own_rows, note)

    own_targets = target.reshape(TB, BLK, E)
    other_targets = other_core(own_targets)
    wide = own_targets.astype(jnp.float32)
    sq_own = jnp.sum(wide * wide, axis=2) * 0.5
    sq_other = other_core(sq_own)
    sq = jnp.where(
        core == 0, jnp.concatenate([sq_own, sq_other]), jnp.concatenate([sq_other, sq_own])
    )
    wide = own_rows.astype(jnp.float32)
    sq_rows = jnp.sum(wide * wide, axis=2)

    here = jnp.stack([chip, core, at_y, at_z]).astype(jnp.int32)
    scratch = [
        pltpu.VMEM((NY, NZ, SB, ROWS, E), jnp.bfloat16),
        pltpu.VMEM((NTGT, BLK, E), jnp.bfloat16),
        pltpu.VMEM((2, ROWS, BLK), jnp.float32),
        pltpu.VMEM((2, ROWS, BLK), jnp.float32),
        pltpu.VMEM((OUT_BUFS, 2, ROWS, BLK), jnp.float32),
        pltpu.VMEM((NZ, NY, NOTE, E), jnp.bfloat16),
        pltpu.VMEM((NY * NZ, 128), jnp.int32),
        pltpu.SMEM((NY * NZ, 128), jnp.int32),
        pltpu.SemaphoreType.DMA((64,)),
        pltpu.SemaphoreType.DMA((OUT_BUFS,)),
    ]
    slots, owns, tiles, tops, lse = call(
        functools.partial(tiles_kernel, 2.0 / epsilon),
        [SMEM, VMEM, ANY, ANY] + [ANY] * 14,
        [
            jax.ShapeDtypeStruct((LIST,), jnp.int32),
            jax.ShapeDtypeStruct((2, 8, 128), jnp.int32),
            f32(NSLOT, ROWS, BLK),
            f32(2, ROWS, 128),
            f32(NSRC, ROWS),
        ],
        [SMEM, VMEM, ANY, VMEM, VMEM],
        [pltpu.VMEM((2, ROWS, 128), jnp.float32), pltpu.VMEM((ROWS, 128), jnp.float32)] + scratch,
        48,
    )(here, sq, own_targets, other_targets, *gathered)

    col, alpha, potential = call(
        first_columns_kernel,
        [SMEM] + [VMEM] * 6 + [ANY],
        [f32(NTGT, BLK), f32(2, ROWS, 128), f32(NSRC, ROWS)],
        [VMEM] * 3,
        stream_scratch(),
        24,
    )(slots, owns, *join_plane(lse, join_lse), tops, tiles)

    row_sum = call(
        rows_kernel,
        [SMEM] + [VMEM] * 5 + [ANY],
        f32(NSRC, ROWS),
        VMEM,
        [pltpu.VMEM((NTGT, BLK), jnp.float32), pltpu.VMEM((ROWS, 128), jnp.float32)]
        + stream_scratch(),
        24,
    )(slots, *from_reps(col + other_core(col)), alpha, tiles)
    row_sum = sum(join_plane(row_sum, sum))

    col = call(
        last_columns_kernel,
        [SMEM, VMEM, VMEM, VMEM, ANY],
        f32(NTGT, BLK),
        VMEM,
        [pltpu.VMEM((2, ROWS, 128), jnp.float32)] + stream_scratch(),
        24,
    )(slots, owns, row_sum, alpha, tiles)

    mine = lax.dynamic_slice_in_dim(potential, chip * SB, SB, 0)
    mine = mine - jnp.log(lax.dynamic_slice_in_dim(row_sum, chip * SB, SB, 0))
    f_part = epsilon * mine + sq_rows

    halves = col.reshape(NCORE, TB, BLK)
    keep = lax.dynamic_index_in_dim(halves, core, 0, False)
    give = lax.dynamic_index_in_dim(halves, 1 - core, 0, False)
    f_line = jnp.pad(f_part.reshape(1, SB * ROWS), ((0, 0), (0, BLK - SB * ROWS)))
    last = from_reps(jnp.concatenate([keep + other_core(give), f_line]))
    col = sum_four([p[:TB] for p in last])
    g_out = -epsilon * jnp.log(col + math.exp(DUSTBIN))
    lines = jnp.stack([p[TB, : SB * ROWS].reshape(SB, ROWS) for p in last])
    f_out = jnp.stack(
        [lax.dynamic_index_in_dim(lines, (rep - j) % NREP, 0, False) for j in range(NREP)], axis=1
    )
    return f_out.reshape(-1), g_out.reshape(-1)


def solution(mesh):
    in_specs = (P("cells", None), P("cells", None), P("cells", "rep"), P("cells"))
    out_specs = (P("cells"), P("cells"))
    return jax.shard_map(body, mesh=mesh, in_specs=in_specs, out_specs=out_specs, check_vma=False)
```
